512 devices in a mesh: row: 16 (over z, y_hi), col: 32 (over y_lo, x, core).
Axes of the slice: x: 4, y: 8 (y_hi: 2, y_lo: 4; y = y_hi * 4 + y_lo), z: 8, core: 2. Of those that a mesh axis runs over, the one named last changes fastest.
Arguments:
- weight_half: bfloat16 [8192, 14336], P('row', 'col'), may hold values from -3 to 3
- weight_full: float32 [8192, 14336], P('row', 'col'), may hold values from -3 to 3
- adapter_b: float32 [2, 8192, 128], P(None, ('row', 'col')), may hold values from -6 to 6
- adapter_a: float32 [2, 128, 14336], P(None, None, ('col', 'row')), may hold values from -1 to 1
- moments_b: float32 [2, 2, 8192, 128], P(None, None, ('row', 'col')), may hold values from 0.01 to 1
- moments_a: float32 [2, 2, 128, 14336], P(None, None, None, ('col', 'row')), may hold values from 0.01 to 1
- reset_rows: int32 [2, 64], replicated, may hold values 0 or 1
- reset_cols: int32 [2, 112], replicated, may hold values 0 or 1
Outputs:
- merged_half: bfloat16 [8192, 14336], P('row', 'col')
- merged_full: float32 [8192, 14336], P('row', 'col')
- restart_b: float32 [2, 2, 8192, 128], P(None, None, ('row', 'col'))
- restart_a: float32 [2, 2, 128, 14336], P(None, None, None, ('col', 'row'))
The draws below stay inside these ranges and needn't reach their ends.
All inputs are finite; a program needn't handle non-finite values.
Results may differ from the reference program's by a relative error of at most 0.001.
Values sent between devices are 32-bit elements; how exact they have to be, the bound alone decides.
A program may use at most 64 MiB of HBM per device.

```python
import math
import jax
import jax.numpy as jnp
from jax import lax

D = 8192
FFN = 14336
RANK = 128
LAYERS = 2
BLOCK = 128


def plant(result, stream_key, smallest, largest):
    longest = result.shape.index(max(result.shape))
    spots = []
    for shift in (0, 1):
        where = [jax.random.randint(jax.random.fold_in(stream_key, axis), (), 0, length) for axis, length in enumerate(result.shape)]
        where[longest] = (where[longest] + shift) % result.shape[longest]
        spots.append(tuple(where))
    return result.at[spots[0]].set(smallest).at[spots[1]].set(largest)


def levels(key, shape, pieces, smallest, top_value):
    def one(axis_at, blocks):
        heights = jax.random.uniform(jax.random.fold_in(jax.random.fold_in(key, 6), axis_at), (blocks,), jnp.float32, smallest / len(pieces), top_value / len(pieces))
        return jnp.repeat(jnp.exp(heights), shape[axis_at] // blocks).reshape((-1,) + (1,) * (len(shape) - axis_at - 1))

    loudness = one(*pieces[0])
    for cut in pieces[1:]:
        loudness = loudness * one(*cut)
    return loudness


def centred(rng, extent, scale, reach, pieces=(), dtype=jnp.bfloat16):
    values = scale * jax.random.normal(rng, extent, jnp.float32)
    if pieces:
        values = values * levels(rng, extent, pieces, -0.22, 0.18)
    return jnp.clip(values, -reach, reach).astype(dtype)


def setup_inputs(seed: int = 0) -> dict:
    keys = jax.random.split(jax.random.key(seed), 9)
    return {
        "weight_half": centred(keys[0], (D, FFN), 0.5, 3.0, ((0, 16), (1, 32))),
        "weight_full": centred(keys[1], (D, FFN), 0.5, 3.0, ((0, 16), (1, 32)), jnp.float32),
        "adapter_b": centred(keys[2], (LAYERS, D, RANK), 1.0, 6.0, ((1, 512),), jnp.float32),
        "adapter_a": centred(keys[3], (LAYERS, RANK, FFN), 0.18, 1.0, ((2, 512),), jnp.float32),
        "moments_b": jnp.clip(jnp.exp(math.log(1.0) - 4.6051702 * jax.random.uniform(keys[4], (LAYERS, 2, D, RANK), jnp.float32) ** levels(keys[4], (LAYERS, 2, D, RANK), ((2, 512),), -0.2, 0.2)), 0.01, 1.0),
        "moments_a": jnp.clip(jnp.exp(math.log(1.0) - 4.6051702 * jax.random.uniform(keys[5], (LAYERS, 2, RANK, FFN), jnp.float32) ** levels(keys[5], (LAYERS, 2, RANK, FFN), ((3, 512),), -0.2, 0.2)), 0.01, 1.0),
        "reset_rows": plant((jax.random.randint(keys[6], (LAYERS, D // BLOCK), 0, 2) < 1).astype(jnp.int32), jax.random.fold_in(keys[6], 1), 0, 1),
        "reset_cols": plant((jax.random.randint(keys[7], (LAYERS, FFN // BLOCK), 0, 2) < 1).astype(jnp.int32), jax.random.fold_in(keys[7], 1), 0, 1),
    }


merge_scale = 0.25


def reference(weight_half, weight_full, adapter_b, adapter_a, moments_b, moments_a, reset_rows, reset_cols):
    def update(layer_index):
        return merge_scale * jnp.dot(adapter_b[layer_index], adapter_a[layer_index], precision=lax.Precision.HIGHEST, preferred_element_type=jnp.float32)

    merged_half = (weight_half.astype(jnp.float32) + update(0)).astype(jnp.bfloat16)
    merged_full = weight_full + update(1)
    row_flags = jnp.repeat(reset_rows, BLOCK, axis=1)
    col_flags = jnp.repeat(reset_cols, BLOCK, axis=1)
    restart_b = jnp.where(row_flags[:, None, :, None] == 1, jnp.zeros_like(moments_b), moments_b)
    restart_a = jnp.where(col_flags[:, None, None, :] == 1, jnp.zeros_like(moments_a), moments_a)
    return merged_half, merged_full, restart_b, restart_a
```

```python
import functools

import jax
import jax.numpy as jnp
from jax import lax
from jax.experimental import pallas as pl
from jax.experimental.pallas import tpu as pltpu
from jax.sharding import PartitionSpec as P

LAYERS = 2
BLOCK = 128
MERGE_SCALE = 0.25
MESH = pl.DeviceIdType.MESH
NZ, NH, NY, NX, NC = 8, 2, 4, 4, 2
REACH = {(1, 0): 4, (-1, 0): 3, (1, 1): 3, (-1, 1): 4}

A_PARTNER = 0
A_CHAIN = {}
for _key, _reach in REACH.items():
    for _d in range(1, _reach + 1):
        A_CHAIN[_key + (_d,)] = 1 + len(A_CHAIN)
B_LINE = {k: 1 + len(A_CHAIN) + k - 1 for k in range(1, NY)}
_next = 1 + len(A_CHAIN) + len(B_LINE)
B_NEAR = {1: _next, -1: _next + 1}
B_FAR = {1: _next + 2, -1: _next + 3}
B_CORE = {0: _next + 4, 1: _next + 5, -1: _next + 6, (2, 1): _next + 7, (2, -1): _next + 8}
MESSAGES = _next + 9


def gather_merge(
    wh_ref, wf_ref, b_ref, a_ref, mb_ref, ma_ref, rr_ref, rc_ref,
    oh_ref, of_ref, ob_ref, oa_ref,
    a_all, b_all, b_cat, row_flags, col_flags, send_sem, recv_sem, local_sem,
):
    row, col = lax.axis_index("row"), lax.axis_index("col")
    z, h = row // NH, row % NH
    y, x, core = col // (NX * NC), (col // NC) % NX, col % NC
    a_rows = a_ref.shape[0]
    b_rows = b_ref.shape[0]
    rows_owned = b_rows // LAYERS
    cols_owned = a_rows // LAYERS

    def dev(dz=0, flip_h=0, ky=0, dx=0, flip_core=0):
        tz = (z + dz + NZ) % NZ
        th = (h + flip_h) % NH
        ty = pair(y, ky)
        tx = (x + dx + NX) % NX
        tc = (core + flip_core) % NC
        return (tz * NH + th, (ty * NX + tx) * NC + tc)

    def pair(v, k):
        low, high = v % 2, v // 2
        return ((high + k // 2) % 2) * 2 + (low + k % 2) % 2

    def a_slot(dz, flip_h):
        pos = ((z + dz + NZ) % NZ) * NH + (h + flip_h) % NH
        return a_all.at[pl.ds(pl.multiple_of(pos * a_rows, 8), a_rows), :]

    def b_slot(dx, y_first, y_count, flip_core=0):
        pos = (((core + flip_core) % NC) * NX + (x + dx + NX) % NX) * NY + y_first
        return b_all.at[pl.ds(pl.multiple_of(pos * b_rows, 8), y_count * b_rows), :]

    local = [
        pltpu.make_async_copy(a_ref, a_slot(0, 0), local_sem.at[0]),
        pltpu.make_async_copy(b_ref, b_slot(0, y, 1), local_sem.at[1]),
        pltpu.make_async_copy(mb_ref, ob_ref, local_sem.at[2]),
        pltpu.make_async_copy(ma_ref, oa_ref, local_sem.at[3]),
        pltpu.make_async_copy(wh_ref, oh_ref, local_sem.at[4]),
        pltpu.make_async_copy(wf_ref, of_ref, local_sem.at[5]),
        pltpu.make_async_copy(rr_ref, row_flags, local_sem.at[6]),
        pltpu.make_async_copy(rc_ref, col_flags, local_sem.at[7]),
    ]
    for c in local:
        c.start()

    barrier = pltpu.get_barrier_semaphore()
    greeted = [dev(flip_h=1), dev(dz=1), dev(dz=-1)]
    greeted += [dev(ky=k) for k in range(1, NY)]
    greeted += [dev(dx=1), dev(dx=-1), dev(flip_core=1)]
    for other in greeted:
        pl.semaphore_signal(barrier, inc=1, device_id=other, device_id_type=MESH)
    pl.semaphore_wait(barrier, len(greeted))

    sent = []

    def send(src, dst, message, device):
        c = pltpu.make_async_remote_copy(
            src_ref=src, dst_ref=dst, send_sem=send_sem.at[message],
            recv_sem=recv_sem.at[message], device_id=device, device_id_type=MESH,
        )
        c.start()
        sent.append(c)

    def arrive(dst, message):
        pltpu.make_async_copy(dst, dst, recv_sem.at[message]).wait()

    def a_send(s, o, d):
        slot = a_slot(-s * (d - 1), o)
        src = a_ref if (d == 1 and o == 0) else slot
        send(src, slot, A_CHAIN[s, o, d], dev(dz=s))

    def a_arrive(s, o, d):
        arrive(a_slot(-s * d, o), A_CHAIN[s, o, d])
        if d < REACH[s, o]:
            a_send(s, o, d + 1)

    send(a_ref, a_slot(0, 0), A_PARTNER, dev(flip_h=1))
    a_send(1, 0, 1)
    a_send(-1, 0, 1)
    for k in range(1, NY):
        send(b_ref, b_slot(0, y, 1), B_LINE[k], dev(ky=k))

    row_first = (row * (NY * NX * NC) + col) * rows_owned
    col_first = (col * (NZ * NH) + row) * cols_owned
    for i in (2, 3, 6, 7):
        local[i].wait()
    column = col_first + lax.broadcasted_iota(jnp.int32, (a_rows, BLOCK), 0) // 2
    first_block = col_first // BLOCK
    last_block = (col_first + cols_owned - 1) // BLOCK
    for l in range(LAYERS):
        keep_b = 1 - row_flags[l, row_first // BLOCK]
        ob_ref[l] = jnp.where(jnp.full(ob_ref.shape[1:], keep_b) == 0, 0.0, ob_ref[l])
        flag = jnp.where(column // BLOCK == first_block, col_flags[l, first_block], col_flags[l, last_block])
        oa_ref[l] = jnp.where(flag == 1, 0.0, oa_ref[l])

    a_arrive(1, 0, 1)
    a_arrive(-1, 0, 1)
    local[0].wait()
    local[1].wait()
    for k in range(1, NY):
        arrive(b_slot(0, pair(y, k), 1), B_LINE[k])
    for s in (1, -1):
        send(b_slot(0, 0, NY), b_slot(0, 0, NY), B_NEAR[s], dev(dx=s))
    send(b_slot(0, 0, NY), b_slot(0, 0, NY), B_CORE[0], dev(flip_core=1))
    arrive(a_slot(0, 1), A_PARTNER)
    a_send(1, 1, 1)
    a_send(-1, 1, 1)
    a_arrive(1, 0, 2)
    a_arrive(-1, 0, 2)
    for s in (1, -1):
        arrive(b_slot(-s, 0, NY), B_NEAR[s])
        half = b_slot(-s, 0 if s == 1 else NY // 2, NY // 2)
        send(half, half, B_FAR[s], dev(dx=s))
        send(b_slot(-s, 0, NY), b_slot(-s, 0, NY), B_CORE[-s], dev(flip_core=1))
    a_arrive(1, 1, 1)
    a_arrive(-1, 1, 1)
    a_arrive(1, 0, 3)
    a_arrive(-1, 0, 3)
    for s in (1, -1):
        half = b_slot(2, 0 if s == 1 else NY // 2, NY // 2)
        arrive(half, B_FAR[s])
        send(half, half, B_CORE[2, s], dev(flip_core=1))
    a_arrive(1, 1, 2)
    a_arrive(-1, 1, 2)
    for dx in (0, 1, -1):
        arrive(b_slot(dx, 0, NY, 1), B_CORE[dx])
    for s in (1, -1):
        arrive(b_slot(2, 0 if s == 1 else NY // 2, NY // 2, 1), B_CORE[2, s])

    def split(v):
        high = v.astype(jnp.bfloat16)
        return high, (v - high.astype(jnp.float32)).astype(jnp.bfloat16)

    for by in range(NY):
        for bx in range(NX):
            for bc in range(NC):
                at = ((bc * NX + bx) * NY + by) * b_rows
                to = ((by * NX + bx) * NC + bc) * rows_owned
                for l in range(LAYERS):
                    high, low = split(b_all[pl.ds(at + l * rows_owned, rows_owned), :])
                    b_cat[l, pl.ds(to, rows_owned), 0:128] = high
                    b_cat[l, pl.ds(to, rows_owned), 128:256] = high
                    b_cat[l, pl.ds(to, rows_owned), 256:384] = low

    a_arrive(1, 1, 3)
    a_arrive(-1, 1, 3)
    a_arrive(1, 0, 4)
    local[4].wait()
    local[5].wait()

    group = 2 * NH * cols_owned

    def merge(dj):
        j = (z // 2 + dj + NZ // 2) % (NZ // 2)
        first = pl.multiple_of(j * group, 16)
        for l, out in ((0, oh_ref), (1, of_ref)):
            high, low = split(a_all[pl.ds(first * 2 + l, group, stride=2), :])
            update = lax.dot_general(
                jnp.concatenate([high, low, high], axis=1), b_cat[l],
                (((1,), (1,)), ((), ())), preferred_element_type=jnp.float32,
            )
            at = (pl.ds(first, group), slice(None))
            out[at] = (out[at].astype(jnp.float32) + MERGE_SCALE * update).astype(out.dtype)

    merge(0)
    merge(1)
    merge(-1)
    a_arrive(-1, 1, 4)
    merge(2)
    for c in sent:
        c.wait_send()


def deliver(*refs):
    sems = refs[-1]
    half = (len(refs) - 1) // 2
    copies = [
        pltpu.make_async_copy(refs[i], refs[half + i], sems.at[i]) for i in range(half)
    ]
    for c in copies:
        c.start()
    for c in copies:
        c.wait()


def per_device(
    weight_half, weight_full, adapter_b, adapter_a, moments_b, moments_a, reset_rows, reset_cols
):
    layers, rows_owned, rank = adapter_b.shape
    cols_owned = adapter_a.shape[2]
    wh, wf = weight_half.T, weight_full.T
    b = adapter_b.reshape(layers * rows_owned, rank)
    a = adapter_a.transpose(2, 0, 1).reshape(cols_owned * layers, rank)
    mb = moments_b.reshape(layers, 2 * rows_owned, rank)
    ma = moments_a.transpose(0, 3, 1, 2).reshape(layers, cols_owned * 2, rank)
    shapes = [wh, wf, mb, ma]
    hbm = pl.BlockSpec(memory_space=pl.ANY)
    vmem = pl.BlockSpec(memory_space=pltpu.VMEM)
    merged = pl.pallas_call(
        gather_merge,
        name="gather_merge",
        out_shape=[pltpu.VMEM(s.shape, s.dtype) for s in shapes],
        in_specs=[hbm] * 8,
        out_specs=[vmem] * 4,
        scratch_shapes=[
            pltpu.VMEM((NZ * NH * a.shape[0], rank), jnp.float32),
            pltpu.VMEM((NY * NX * NC * b.shape[0], rank), jnp.float32),
            pltpu.VMEM((layers, NY * NX * NC * rows_owned, 3 * rank), jnp.bfloat16),
            pltpu.SMEM(reset_rows.shape, jnp.int32),
            pltpu.SMEM(reset_cols.shape, jnp.int32),
            pltpu.SemaphoreType.DMA((MESSAGES,)),
            pltpu.SemaphoreType.DMA((MESSAGES,)),
            pltpu.SemaphoreType.DMA((8,)),
        ],
        compiler_params=pltpu.CompilerParams(
            collective_id=0, has_side_effects=True, vmem_limit_bytes=32 * 1024 * 1024
        ),
    )(*(
        pltpu.with_memory_space_constraint(v, pltpu.HBM)
        for v in (wh, wf, b, a, mb, ma, reset_rows, reset_cols)
    ))
    merged = [pltpu.with_memory_space_constraint(m, pltpu.VMEM) for m in merged]
    oh, of, ob, oa = pl.pallas_call(
        deliver,
        name="deliver",
        out_shape=[jax.ShapeDtypeStruct(s.shape, s.dtype) for s in shapes],
        in_specs=[vmem] * 4,
        out_specs=[hbm] * 4,
        scratch_shapes=[pltpu.SemaphoreType.DMA((4,))],
    )(*merged)
    oa = oa.reshape(layers, cols_owned, 2, rank).transpose(0, 2, 3, 1)
    return oh.T, of.T, ob.reshape(moments_b.shape), oa


def solution(mesh):
    return jax.shard_map(
        per_device,
        mesh=mesh,
        in_specs=(
            P("row", "col"),
            P("row", "col"),
            P(None, ("row", "col"), None),
            P(None, None, ("col", "row")),
            P(None, None, ("row", "col"), None),
            P(None, None, None, ("col", "row")),
            P(),
            P(),
        ),
        out_specs=(
            P("row", "col"),
            P("row", "col"),
            P(None, None, ("row", "col"), None),
            P(None, None, None, ("col", "row")),
        ),
        check_vma=False,
    )
```

```python
import functools

import jax
import jax.numpy as jnp
from jax import lax
from jax.experimental import pallas as pl
from jax.experimental.pallas import tpu as pltpu
from jax.sharding import PartitionSpec as P

LAYERS = 2
BLOCK = 128
MERGE_SCALE = 0.25
MESH = pl.DeviceIdType.MESH
NZ, NH, NY, NX, NC = 8, 2, 4, 4, 2
X_STEPS = (2, 1, -1)
A_PARTNER = 0
A_Z = 1
B_FIRST = A_Z + NH * NZ
B_LINE = {k: B_FIRST + k for k in range(1, NY)}
B_X = {d: B_FIRST + NY + i for i, d in enumerate(X_STEPS)}
B_CORE = {d: B_FIRST + NY + len(X_STEPS) + i for i, d in enumerate((0, *X_STEPS))}
MESSAGES = B_FIRST + NY + 2 * len(X_STEPS) + 1


def gather_merge(
    wh_ref, wf_ref, b_ref, a_ref, mb_ref, ma_ref, rr_ref, rc_ref,
    oh_ref, of_ref, ob_ref, oa_ref,
    a_all, b_all, b_cat, row_flags, col_flags, send_sem, recv_sem, local_sem, ready_sem,
):
    row, col = lax.axis_index("row"), lax.axis_index("col")
    z, h = row // NH, row % NH
    y, x, core = col // (NX * NC), (col // NC) % NX, col % NC
    a_rows = a_ref.shape[0]
    b_rows = b_ref.shape[0]
    rows_owned = b_rows // LAYERS
    cols_owned = a_rows // LAYERS

    def dev(dz=0, flip_h=0, ky=0, dx=0, flip_core=0):
        tz = (z + dz + NZ) % NZ
        th = (h + flip_h) % NH
        ty = pair(y, ky)
        tx = (x + dx + NX) % NX
        tc = (core + flip_core) % NC
        return (tz * NH + th, (ty * NX + tx) * NC + tc)

    def pair(v, k):
        low, high = v % 2, v // 2
        return ((high + k // 2) % 2) * 2 + (low + k % 2) % 2

    def at_z(t):
        return (t * NH + h, col)

    def a_slot(t, flip_h):
        pos = t * NH + (h + flip_h) % NH
        return a_all.at[pl.ds(pl.multiple_of(pos * a_rows, 8), a_rows), :]

    def b_slot(dx, y_first, y_count, flip_core=0):
        pos = (((core + flip_core) % NC) * NX + (x + dx + NX) % NX) * NY + y_first
        return b_all.at[pl.ds(pl.multiple_of(pos * b_rows, 8), y_count * b_rows), :]

    barrier = pltpu.get_barrier_semaphore()

    def greet(other):
        pl.semaphore_signal(barrier, inc=1, device_id=other, device_id_type=MESH)

    def order_y(v):
        return v + h * (NY - 1 - 2 * v)

    def y_later(k):
        return order_y(pair(y, k)) > order_y(y)

    def x_later(d):
        return (x + d + NX) % NX > x

    def when(condition, action):
        pl.when(condition)(action)

    for t in range(1, NZ):
        when(t > z, functools.partial(greet, at_z(t)))
    when(h == 0, functools.partial(greet, dev(flip_h=1)))
    for k in range(1, NY):
        when(y_later(k), functools.partial(greet, dev(ky=k)))
    for d in X_STEPS:
        when(x_later(d), functools.partial(greet, dev(dx=d)))
    when(core == 1, functools.partial(greet, dev(flip_core=1)))

    def tell(number, other):
        pl.semaphore_signal(ready_sem.at[number], inc=1, device_id=other, device_id_type=MESH)

    def told(number):
        pl.semaphore_wait(ready_sem.at[number], 1)

    greetings = z + h + order_y(y) + x + 1 - core

    @pl.when(greetings > 0)
    def _():
        pl.semaphore_wait(barrier, greetings)

    def message(src, dst, number, device):
        return pltpu.make_async_remote_copy(
            src_ref=src, dst_ref=dst, send_sem=send_sem.at[number],
            recv_sem=recv_sem.at[number], device_id=device, device_id_type=MESH,
        )

    def arrive(dst, number):
        pltpu.make_async_copy(dst, dst, recv_sem.at[number]).wait()

    def a_message(o, t):
        slot = a_slot(z, o)
        return message(slot if o else a_ref, slot, A_Z + o * NZ + (t - z + NZ) % NZ, at_z(t))

    def a_arrive(o, t):
        arrive(a_slot(t, o), A_Z + o * NZ + (z - t + NZ) % NZ)

    partner = message(a_ref, a_slot(z, 0), A_PARTNER, dev(flip_h=1))
    b_line = {k: message(b_ref, b_slot(0, y, 1), B_LINE[k], dev(ky=k)) for k in range(1, NY)}

    @pl.when(h == 1)
    def _():
        partner.start()
        tell(A_PARTNER, dev(flip_h=1))

    for t in range(NZ - 1):
        @pl.when(t < z)
        def _():
            a_message(0, t).start()
            tell(A_Z + (t - z + NZ) % NZ, at_z(t))

    for k, c in b_line.items():
        @pl.when(jnp.logical_not(y_later(k)))
        def _():
            c.start()
            tell(B_LINE[k], dev(ky=k))

    for d in X_STEPS:
        @pl.when(jnp.logical_not(x_later(d)))
        def _():
            tell(B_X[d], dev(dx=d))

    @pl.when(core == 0)
    def _():
        tell(B_CORE[0], dev(flip_core=1))

    local = [
        pltpu.make_async_copy(a_ref, a_slot(z, 0), local_sem.at[0]),
        pltpu.make_async_copy(b_ref, b_slot(0, y, 1), local_sem.at[1]),
        pltpu.make_async_copy(mb_ref, ob_ref, local_sem.at[2]),
        pltpu.make_async_copy(ma_ref, oa_ref, local_sem.at[3]),
        pltpu.make_async_copy(wh_ref, oh_ref, local_sem.at[4]),
        pltpu.make_async_copy(wf_ref, of_ref, local_sem.at[5]),
        pltpu.make_async_copy(rr_ref, row_flags, local_sem.at[6]),
        pltpu.make_async_copy(rc_ref, col_flags, local_sem.at[7]),
    ]
    for c in local:
        c.start()

    row_first = (row * (NY * NX * NC) + col) * rows_owned
    col_first = (col * (NZ * NH) + row) * cols_owned
    for i in (2, 3, 6, 7):
        local[i].wait()
    column = col_first + lax.broadcasted_iota(jnp.int32, (a_rows, BLOCK), 0) // 2
    first_block = col_first // BLOCK
    last_block = (col_first + cols_owned - 1) // BLOCK
    for l in range(LAYERS):
        keep_b = 1 - row_flags[l, row_first // BLOCK]
        ob_ref[l] = jnp.where(jnp.full(ob_ref.shape[1:], keep_b) == 0, 0.0, ob_ref[l])
        flag = jnp.where(column // BLOCK == first_block, col_flags[l, first_block], col_flags[l, last_block])
        oa_ref[l] = jnp.where(flag == 1, 0.0, oa_ref[l])

    @pl.when(h == 0)
    def _():
        told(A_PARTNER)
        partner.start()

    for k, c in b_line.items():
        @pl.when(y_later(k))
        def _():
            told(B_LINE[k])
            c.start()

    local[0].wait()
    local[1].wait()
    for k in range(1, NY):
        arrive(b_slot(0, pair(y, k), 1), B_LINE[k])
    b_group = b_slot(0, 0, NY)
    b_near = {d: message(b_group, b_group, B_X[d], dev(dx=d)) for d in X_STEPS}
    for d, c in b_near.items():
        @pl.when(x_later(d))
        def _():
            told(B_X[d if 2 * d == NX else -d])

        c.start()

    @pl.when(core == 1)
    def _():
        told(B_CORE[0])

    b_shared = [message(b_group, b_group, B_CORE[0], dev(flip_core=1))]
    b_shared[0].start()

    @pl.when(h == 0)
    def _():
        arrive(a_slot(z, 1), A_PARTNER)
        for t in range(NZ - 1):
            @pl.when(t < z)
            def _():
                a_message(1, t).start()

    for t in range(1, NZ):
        @pl.when(t > z)
        def _():
            told(A_Z + (z - t + NZ) % NZ)
            a_message(0, t).start()

            @pl.when(h == 0)
            def _():
                a_message(1, t).start()

    @pl.when(h == 1)
    def _():
        arrive(a_slot(z, 1), A_PARTNER)
        for t in range(NZ):
            @pl.when(t != z)
            def _():
                a_message(1, t).start()

    for d in X_STEPS[::-1]:
        group_b = b_slot(-d, 0, NY)
        arrive(group_b, B_X[d])
        b_shared.append(message(group_b, group_b, B_CORE[d], dev(flip_core=1)))
        b_shared[-1].start()
    for d in (0, *X_STEPS[::-1]):
        arrive(b_slot(-d, 0, NY, 1), B_CORE[d])

    def split(v):
        high = v.astype(jnp.bfloat16)
        return high, (v - high.astype(jnp.float32)).astype(jnp.bfloat16)

    for by in range(NY):
        for bx in range(NX):
            for bc in range(NC):
                at = ((bc * NX + bx) * NY + by) * b_rows
                to = ((by * NX + bx) * NC + bc) * rows_owned
                for l in range(LAYERS):
                    high, low = split(b_all[pl.ds(at + l * rows_owned, rows_owned), :])
                    b_cat[l, pl.ds(to, rows_owned), 0:128] = high
                    b_cat[l, pl.ds(to, rows_owned), 128:256] = high
                    b_cat[l, pl.ds(to, rows_owned), 256:384] = low

    local[4].wait()
    local[5].wait()

    group = 2 * NH * cols_owned

    def merge(j):
        first = pl.multiple_of(j * group, 16)
        for l, out in ((0, oh_ref), (1, of_ref)):
            high, low = split(a_all[pl.ds(first * 2 + l, group, stride=2), :])
            update = lax.dot_general(
                jnp.concatenate([high, low, high], axis=1), b_cat[l],
                (((1,), (1,)), ((), ())), preferred_element_type=jnp.float32,
            )
            at = (pl.ds(first, group), slice(None))
            out[at] = (out[at].astype(jnp.float32) + MERGE_SCALE * update).astype(out.dtype)

    for t in range(NZ):
        @pl.when(t != z)
        def _():
            a_arrive(0, t)

    def partner_pair(dj):
        j = (z // 2 + dj + NZ // 2) % (NZ // 2)
        for t in (2 * j, 2 * j + 1):
            @pl.when(t != z)
            def _():
                a_arrive(1, t)
        merge(j)

    for dj in (0, 1, -1, 2):
        partner_pair(dj)

    sent = [partner, *b_line.values(), *b_near.values(), *b_shared]
    for t in range(NZ):
        @pl.when(t != z)
        def _():
            for o in range(NH):
                a_message(o, t).wait_send()
    for c in sent:
        c.wait_send()


def deliver(*refs):
    sems = refs[-1]
    half = (len(refs) - 1) // 2
    copies = [
        pltpu.make_async_copy(refs[i], refs[half + i], sems.at[i]) for i in range(half)
    ]
    for c in copies:
        c.start()
    for c in copies:
        c.wait()


def per_device(
    weight_half, weight_full, adapter_b, adapter_a, moments_b, moments_a, reset_rows, reset_cols
):
    layers, rows_owned, rank = adapter_b.shape
    cols_owned = adapter_a.shape[2]
    wh, wf = weight_half.T, weight_full.T
    b = adapter_b.reshape(layers * rows_owned, rank)
    a = adapter_a.transpose(2, 0, 1).reshape(cols_owned * layers, rank)
    mb = moments_b.reshape(layers, 2 * rows_owned, rank)
    ma = moments_a.transpose(0, 3, 1, 2).reshape(layers, cols_owned * 2, rank)
    shapes = [wh, wf, mb, ma]
    hbm = pl.BlockSpec(memory_space=pl.ANY)
    vmem = pl.BlockSpec(memory_space=pltpu.VMEM)
    merged = pl.pallas_call(
        gather_merge,
        name="gather_merge",
        out_shape=[pltpu.VMEM(s.shape, s.dtype) for s in shapes],
        in_specs=[hbm] * 8,
        out_specs=[vmem] * 4,
        scratch_shapes=[
            pltpu.VMEM((NZ * NH * a.shape[0], rank), jnp.float32),
            pltpu.VMEM((NY * NX * NC * b.shape[0], rank), jnp.float32),
            pltpu.VMEM((layers, NY * NX * NC * rows_owned, 3 * rank), jnp.bfloat16),
            pltpu.SMEM(reset_rows.shape, jnp.int32),
            pltpu.SMEM(reset_cols.shape, jnp.int32),
            pltpu.SemaphoreType.DMA((MESSAGES,)),
            pltpu.SemaphoreType.DMA((MESSAGES,)),
            pltpu.SemaphoreType.DMA((8,)),
            pltpu.SemaphoreType.REGULAR((B_X[X_STEPS[-1]] + 2,)),
        ],
        compiler_params=pltpu.CompilerParams(
            collective_id=0, has_side_effects=True, vmem_limit_bytes=32 * 1024 * 1024
        ),
    )(*(
        pltpu.with_memory_space_constraint(v, pltpu.HBM)
        for v in (wh, wf, b, a, mb, ma, reset_rows, reset_cols)
    ))
    merged = [pltpu.with_memory_space_constraint(m, pltpu.VMEM) for m in merged]
    oh, of, ob, oa = pl.pallas_call(
        deliver,
        name="deliver",
        out_shape=[jax.ShapeDtypeStruct(s.shape, s.dtype) for s in shapes],
        in_specs=[vmem] * 4,
        out_specs=[hbm] * 4,
        scratch_shapes=[pltpu.SemaphoreType.DMA((4,))],
    )(*merged)
    oa = oa.reshape(layers, cols_owned, 2, rank).transpose(0, 2, 3, 1)
    return oh.T, of.T, ob.reshape(moments_b.shape), oa


def solution(mesh):
    return jax.shard_map(
        per_device,
        mesh=mesh,
        in_specs=(
            P("row", "col"),
            P("row", "col"),
            P(None, ("row", "col"), None),
            P(None, None, ("col", "row")),
            P(None, None, ("row", "col"), None),
            P(None, None, None, ("col", "row")),
            P(),
            P(),
        ),
        out_specs=(
            P("row", "col"),
            P("row", "col"),
            P(None, None, ("row", "col"), None),
            P(None, None, None, ("col", "row")),
        ),
        check_vma=False,
    )
```

```python
import functools

import jax
import jax.numpy as jnp
from jax import lax
from jax.experimental import pallas as pl
from jax.experimental.pallas import tpu as pltpu
from jax.sharding import PartitionSpec as P

LAYERS = 2
BLOCK = 128
MERGE_SCALE = 0.25
MESH = pl.DeviceIdType.MESH
NZ, NH, NY, NX, NC = 8, 2, 4, 4, 2
X_STEPS = (2, 1, -1)
FAR = 3
A_PARTNER = 0
A_Z = 1
B_FIRST = A_Z + NH * NZ
B_LINE = {k: B_FIRST + k for k in range(1, NY)}
B_X = {d: B_FIRST + NY + i for i, d in enumerate(X_STEPS)}
B_CORE = {d: B_FIRST + NY + len(X_STEPS) + i for i, d in enumerate((0, *X_STEPS))}
MESSAGES = B_FIRST + NY + 2 * len(X_STEPS) + 1


def gather_merge(
    wh_ref, wf_ref, b_ref, a_ref, mb_ref, ma_ref, rr_ref, rc_ref,
    oh_ref, of_ref, ob_ref, oa_ref,
    a_all, b_all, b_cat, row_flags, col_flags, send_sem, recv_sem, local_sem, ready_sem,
):
    row, col = lax.axis_index("row"), lax.axis_index("col")
    z, h = row // NH, row % NH
    y, x, core = col // (NX * NC), (col // NC) % NX, col % NC
    a_rows = a_ref.shape[0]
    b_rows = b_ref.shape[0]
    rows_owned = b_rows // LAYERS
    cols_owned = a_rows // LAYERS

    def dev(dz=0, flip_h=0, ky=0, dx=0, flip_core=0):
        tz = (z + dz + NZ) % NZ
        th = (h + flip_h) % NH
        ty = pair(y, ky)
        tx = (x + dx + NX) % NX
        tc = (core + flip_core) % NC
        return (tz * NH + th, (ty * NX + tx) * NC + tc)

    def pair(v, k):
        low, high = v % 2, v // 2
        return ((high + k // 2) % 2) * 2 + (low + k % 2) % 2

    def at_z(t):
        return (t * NH + h, col)

    def a_slot(t, flip_h):
        pos = t * NH + (h + flip_h) % NH
        return a_all.at[pl.ds(pl.multiple_of(pos * a_rows, 8), a_rows), :]

    def b_slot(dx, y_first, y_count, flip_core=0):
        pos = (((core + flip_core) % NC) * NX + (x + dx + NX) % NX) * NY + y_first
        return b_all.at[pl.ds(pl.multiple_of(pos * b_rows, 8), y_count * b_rows), :]

    barrier = pltpu.get_barrier_semaphore()

    def greet(other):
        pl.semaphore_signal(barrier, inc=1, device_id=other, device_id_type=MESH)

    def order_y(v):
        return v + h * (NY - 1 - 2 * v)

    def y_later(k):
        return order_y(pair(y, k)) > order_y(y)

    def x_later(d):
        return (x + d + NX) % NX > x

    def when(condition, action):
        pl.when(condition)(action)

    for t in range(1, NZ):
        when(t > z, functools.partial(greet, at_z(t)))
    when(h == 0, functools.partial(greet, dev(flip_h=1)))
    for k in range(1, NY):
        when(y_later(k), functools.partial(greet, dev(ky=k)))
    for d in X_STEPS:
        when(x_later(d), functools.partial(greet, dev(dx=d)))
    when(core == 1, functools.partial(greet, dev(flip_core=1)))

    def tell(number, other):
        pl.semaphore_signal(ready_sem.at[number], inc=1, device_id=other, device_id_type=MESH)

    def told(number):
        pl.semaphore_wait(ready_sem.at[number], 1)

    greetings = z + h + order_y(y) + x + 1 - core

    @pl.when(greetings > 0)
    def _():
        pl.semaphore_wait(barrier, greetings)

    def message(src, dst, number, device):
        return pltpu.make_async_remote_copy(
            src_ref=src, dst_ref=dst, send_sem=send_sem.at[number],
            recv_sem=recv_sem.at[number], device_id=device, device_id_type=MESH,
        )

    def arrive(dst, number):
        pltpu.make_async_copy(dst, dst, recv_sem.at[number]).wait()

    def a_message(o, t):
        slot = a_slot(z, o)
        return message(slot if o else a_ref, slot, A_Z + o * NZ + (t - z + NZ) % NZ, at_z(t))

    def a_arrive(o, t):
        arrive(a_slot(t, o), A_Z + o * NZ + (z - t + NZ) % NZ)

    partner = message(a_ref, a_slot(z, 0), A_PARTNER, dev(flip_h=1))
    b_line = {k: message(b_ref, b_slot(0, y, 1), B_LINE[k], dev(ky=k)) for k in range(1, NY)}

    @pl.when(h == 1)
    def _():
        partner.start()
        tell(A_PARTNER, dev(flip_h=1))

    for t in range(NZ - 1):
        @pl.when(t < z)
        def _():
            a_message(0, t).start()
            tell(A_Z + (t - z + NZ) % NZ, at_z(t))

    for k, c in b_line.items():
        @pl.when(jnp.logical_not(y_later(k)))
        def _():
            c.start()
            tell(B_LINE[k], dev(ky=k))

    for d in X_STEPS:
        @pl.when(jnp.logical_not(x_later(d)))
        def _():
            tell(B_X[d], dev(dx=d))

    @pl.when(core == 0)
    def _():
        tell(B_CORE[0], dev(flip_core=1))

    local = [
        pltpu.make_async_copy(a_ref, a_slot(z, 0), local_sem.at[0]),
        pltpu.make_async_copy(b_ref, b_slot(0, y, 1), local_sem.at[1]),
        pltpu.make_async_copy(mb_ref, ob_ref, local_sem.at[2]),
        pltpu.make_async_copy(ma_ref, oa_ref, local_sem.at[3]),
        pltpu.make_async_copy(wh_ref, oh_ref, local_sem.at[4]),
        pltpu.make_async_copy(wf_ref, of_ref, local_sem.at[5]),
        pltpu.make_async_copy(rr_ref, row_flags, local_sem.at[6]),
        pltpu.make_async_copy(rc_ref, col_flags, local_sem.at[7]),
    ]
    for c in local:
        c.start()

    row_first = (row * (NY * NX * NC) + col) * rows_owned
    col_first = (col * (NZ * NH) + row) * cols_owned
    for i in (2, 3, 6, 7):
        local[i].wait()
    column = col_first + lax.broadcasted_iota(jnp.int32, (a_rows, BLOCK), 0) // 2
    first_block = col_first // BLOCK
    last_block = (col_first + cols_owned - 1) // BLOCK
    for l in range(LAYERS):
        keep_b = 1 - row_flags[l, row_first // BLOCK]
        ob_ref[l] = jnp.where(jnp.full(ob_ref.shape[1:], keep_b) == 0, 0.0, ob_ref[l])
        flag = jnp.where(column // BLOCK == first_block, col_flags[l, first_block], col_flags[l, last_block])
        oa_ref[l] = jnp.where(flag == 1, 0.0, oa_ref[l])

    @pl.when(h == 0)
    def _():
        told(A_PARTNER)
        partner.start()

    for k, c in b_line.items():
        @pl.when(y_later(k))
        def _():
            told(B_LINE[k])
            c.start()

    local[0].wait()
    local[1].wait()
    for k in range(1, NY):
        arrive(b_slot(0, pair(y, k), 1), B_LINE[k])
    b_group = b_slot(0, 0, NY)
    b_near = {d: message(b_group, b_group, B_X[d], dev(dx=d)) for d in X_STEPS}
    for d, c in b_near.items():
        @pl.when(x_later(d))
        def _():
            told(B_X[d if 2 * d == NX else -d])

        c.start()

    @pl.when(core == 1)
    def _():
        told(B_CORE[0])

    b_shared = [message(b_group, b_group, B_CORE[0], dev(flip_core=1))]
    b_shared[0].start()

    def far(t):
        steps = (t - z + NZ) % NZ
        return jnp.logical_and(steps >= FAR, steps <= NZ - FAR)

    def close(t):
        return jnp.logical_and(t != z, jnp.logical_not(far(t)))

    def a_crossing(t):
        slot = a_slot(t, 0)
        return message(slot, slot, A_Z + NZ + (z - t + NZ) % NZ, dev(flip_h=1))

    @pl.when(h == 0)
    def _():
        arrive(a_slot(z, 1), A_PARTNER)
        for t in range(NZ - 1):
            @pl.when(jnp.logical_and(t < z, close(t)))
            def _():
                a_message(1, t).start()

    for t in range(1, NZ):
        @pl.when(t > z)
        def _():
            told(A_Z + (z - t + NZ) % NZ)
            a_message(0, t).start()

            @pl.when(jnp.logical_and(h == 0, close(t)))
            def _():
                a_message(1, t).start()

    @pl.when(h == 1)
    def _():
        arrive(a_slot(z, 1), A_PARTNER)
        for t in range(NZ):
            @pl.when(close(t))
            def _():
                a_message(1, t).start()

    for t in range(NZ):
        @pl.when(far(t))
        def _():
            a_arrive(0, t)
            a_crossing(t).start()

    for d in X_STEPS[::-1]:
        group_b = b_slot(-d, 0, NY)
        arrive(group_b, B_X[d])
        b_shared.append(message(group_b, group_b, B_CORE[d], dev(flip_core=1)))
        b_shared[-1].start()

    for d in (0, *X_STEPS[::-1]):
        arrive(b_slot(-d, 0, NY, 1), B_CORE[d])

    def split(v):
        high = v.astype(jnp.bfloat16)
        return high, (v - high.astype(jnp.float32)).astype(jnp.bfloat16)

    for by in range(NY):
        for bx in range(NX):
            for bc in range(NC):
                at = ((bc * NX + bx) * NY + by) * b_rows
                to = ((by * NX + bx) * NC + bc) * rows_owned
                for l in range(LAYERS):
                    high, low = split(b_all[pl.ds(at + l * rows_owned, rows_owned), :])
                    b_cat[l, pl.ds(to, rows_owned), 0:128] = high
                    b_cat[l, pl.ds(to, rows_owned), 128:256] = high
                    b_cat[l, pl.ds(to, rows_owned), 256:384] = low

    local[4].wait()
    local[5].wait()

    group = 2 * NH * cols_owned

    def merge(j):
        first = pl.multiple_of(j * group, 16)
        for l, out in ((0, oh_ref), (1, of_ref)):
            high, low = split(a_all[pl.ds(first * 2 + l, group, stride=2), :])
            update = lax.dot_general(
                jnp.concatenate([high, low, high], axis=1), b_cat[l],
                (((1,), (1,)), ((), ())), preferred_element_type=jnp.float32,
            )
            at = (pl.ds(first, group), slice(None))
            out[at] = (out[at].astype(jnp.float32) + MERGE_SCALE * update).astype(out.dtype)

    for t in range(NZ):
        @pl.when(close(t))
        def _():
            a_arrive(0, t)

    def partner_pair(dj):
        j = (z // 2 + dj + NZ // 2) % (NZ // 2)
        for t in (2 * j, 2 * j + 1):
            @pl.when(t != z)
            def _():
                a_arrive(1, t)
        merge(j)

    for dj in (0, 1, -1, 2):
        partner_pair(dj)

    sent = [partner, *b_line.values(), *b_near.values(), *b_shared]
    for t in range(NZ):
        @pl.when(t != z)
        def _():
            a_message(0, t).wait_send()

        @pl.when(close(t))
        def _():
            a_message(1, t).wait_send()

        @pl.when(far(t))
        def _():
            a_crossing(t).wait_send()
    for c in sent:
        c.wait_send()


def deliver(*refs):
    sems = refs[-1]
    half = (len(refs) - 1) // 2
    copies = [
        pltpu.make_async_copy(refs[i], refs[half + i], sems.at[i]) for i in range(half)
    ]
    for c in copies:
        c.start()
    for c in copies:
        c.wait()


def per_device(
    weight_half, weight_full, adapter_b, adapter_a, moments_b, moments_a, reset_rows, reset_cols
):
    layers, rows_owned, rank = adapter_b.shape
    cols_owned = adapter_a.shape[2]
    wh, wf = weight_half.T, weight_full.T
    b = adapter_b.reshape(layers * rows_owned, rank)
    a = adapter_a.transpose(2, 0, 1).reshape(cols_owned * layers, rank)
    mb = moments_b.reshape(layers, 2 * rows_owned, rank)
    ma = moments_a.transpose(0, 3, 1, 2).reshape(layers, cols_owned * 2, rank)
    shapes = [wh, wf, mb, ma]
    hbm = pl.BlockSpec(memory_space=pl.ANY)
    vmem = pl.BlockSpec(memory_space=pltpu.VMEM)
    merged = pl.pallas_call(
        gather_merge,
        name="gather_merge",
        out_shape=[pltpu.VMEM(s.shape, s.dtype) for s in shapes],
        in_specs=[hbm] * 8,
        out_specs=[vmem] * 4,
        scratch_shapes=[
            pltpu.VMEM((NZ * NH * a.shape[0], rank), jnp.float32),
            pltpu.VMEM((NY * NX * NC * b.shape[0], rank), jnp.float32),
            pltpu.VMEM((layers, NY * NX * NC * rows_owned, 3 * rank), jnp.bfloat16),
            pltpu.SMEM(reset_rows.shape, jnp.int32),
            pltpu.SMEM(reset_cols.shape, jnp.int32),
            pltpu.SemaphoreType.DMA((MESSAGES,)),
            pltpu.SemaphoreType.DMA((MESSAGES,)),
            pltpu.SemaphoreType.DMA((8,)),
            pltpu.SemaphoreType.REGULAR((B_X[X_STEPS[-1]] + 2,)),
        ],
        compiler_params=pltpu.CompilerParams(
            collective_id=0, has_side_effects=True, vmem_limit_bytes=32 * 1024 * 1024
        ),
    )(*(
        pltpu.with_memory_space_constraint(v, pltpu.HBM)
        for v in (wh, wf, b, a, mb, ma, reset_rows, reset_cols)
    ))
    merged = [pltpu.with_memory_space_constraint(m, pltpu.VMEM) for m in merged]
    oh, of, ob, oa = pl.pallas_call(
        deliver,
        name="deliver",
        out_shape=[jax.ShapeDtypeStruct(s.shape, s.dtype) for s in shapes],
        in_specs=[vmem] * 4,
        out_specs=[hbm] * 4,
        scratch_shapes=[pltpu.SemaphoreType.DMA((4,))],
    )(*merged)
    oa = oa.reshape(layers, cols_owned, 2, rank).transpose(0, 2, 3, 1)
    return oh.T, of.T, ob.reshape(moments_b.shape), oa


def solution(mesh):
    return jax.shard_map(
        per_device,
        mesh=mesh,
        in_specs=(
            P("row", "col"),
            P("row", "col"),
            P(None, ("row", "col"), None),
            P(None, None, ("col", "row")),
            P(None, None, ("row", "col"), None),
            P(None, None, None, ("col", "row")),
            P(),
            P(),
        ),
        out_specs=(
            P("row", "col"),
            P("row", "col"),
            P(None, None, ("row", "col"), None),
            P(None, None, None, ("col", "row")),
        ),
        check_vma=False,
    )
```

```python
import functools

import jax
import jax.numpy as jnp
from jax import lax
from jax.experimental import pallas as pl
from jax.experimental.pallas import tpu as pltpu
from jax.sharding import PartitionSpec as P

LAYERS = 2
BLOCK = 128
MERGE_SCALE = 0.25
MESH = pl.DeviceIdType.MESH
NZ, NH, NY, NX, NC = 8, 2, 4, 4, 2
X_STEPS = (2, 1, -1)
FAR = 3
A_PARTNER = 0
A_Z = 1
B_FIRST = A_Z + NH * NZ
B_LINE = {k: B_FIRST + k for k in range(1, NY)}
B_X = {d: B_FIRST + NY + i for i, d in enumerate(X_STEPS)}
B_CORE = {d: B_FIRST + NY + len(X_STEPS) + i for i, d in enumerate((0, *X_STEPS))}
MESSAGES = B_FIRST + NY + 2 * len(X_STEPS) + 1


def split(v):
    high = v.astype(jnp.bfloat16)
    return high, (v - high.astype(jnp.float32)).astype(jnp.bfloat16)


def merge(weight, a_rows, b_split):
    high, low = split(a_rows)
    update = lax.dot_general(
        jnp.concatenate([high, low, high], axis=1), b_split,
        (((1,), (1,)), ((), ())), preferred_element_type=jnp.float32,
    )
    return (weight.astype(jnp.float32) + MERGE_SCALE * update).astype(weight.dtype)


def gather_merge(
    wh_ref, wf_ref, b_ref, a_ref, mb_ref, ma_ref, rr_ref, rc_ref,
    oh_ref, of_ref, ob_ref, oa_ref, b_cat, a_last,
    a_all, b_all, row_flags, col_flags, send_sem, recv_sem, local_sem, ready_sem,
):
    row, col = lax.axis_index("row"), lax.axis_index("col")
    z, h = row // NH, row % NH
    y, x, core = col // (NX * NC), (col // NC) % NX, col % NC
    a_rows = a_ref.shape[0]
    b_rows = b_ref.shape[0]
    rows_owned = b_rows // LAYERS
    cols_owned = a_rows // LAYERS

    def dev(dz=0, flip_h=0, ky=0, dx=0, flip_core=0):
        tz = (z + dz + NZ) % NZ
        th = (h + flip_h) % NH
        ty = pair(y, ky)
        tx = (x + dx + NX) % NX
        tc = (core + flip_core) % NC
        return (tz * NH + th, (ty * NX + tx) * NC + tc)

    def pair(v, k):
        low, high = v % 2, v // 2
        return ((high + k // 2) % 2) * 2 + (low + k % 2) % 2

    def at_z(t):
        return (t * NH + h, col)

    def a_slot(t, flip_h):
        pos = t * NH + (h + flip_h) % NH
        return a_all.at[pl.ds(pl.multiple_of(pos * a_rows, 8), a_rows), :]

    def b_slot(dx, y_first, y_count, flip_core=0):
        pos = (((core + flip_core) % NC) * NX + (x + dx + NX) % NX) * NY + y_first
        return b_all.at[pl.ds(pl.multiple_of(pos * b_rows, 8), y_count * b_rows), :]

    barrier = pltpu.get_barrier_semaphore()

    def greet(other):
        pl.semaphore_signal(barrier, inc=1, device_id=other, device_id_type=MESH)

    def order_y(v):
        return v + h * (NY - 1 - 2 * v)

    def y_later(k):
        return order_y(pair(y, k)) > order_y(y)

    def x_later(d):
        return (x + d + NX) % NX > x

    def when(condition, action):
        pl.when(condition)(action)

    for t in range(1, NZ):
        when(t > z, functools.partial(greet, at_z(t)))
    when(h == 0, functools.partial(greet, dev(flip_h=1)))
    for k in range(1, NY):
        when(y_later(k), functools.partial(greet, dev(ky=k)))
    for d in X_STEPS:
        when(x_later(d), functools.partial(greet, dev(dx=d)))
    when(core == 1, functools.partial(greet, dev(flip_core=1)))

    def tell(number, other):
        pl.semaphore_signal(ready_sem.at[number], inc=1, device_id=other, device_id_type=MESH)

    def told(number):
        pl.semaphore_wait(ready_sem.at[number], 1)

    greetings = z + h + order_y(y) + x + 1 - core

    @pl.when(greetings > 0)
    def _():
        pl.semaphore_wait(barrier, greetings)

    def message(src, dst, number, device):
        return pltpu.make_async_remote_copy(
            src_ref=src, dst_ref=dst, send_sem=send_sem.at[number],
            recv_sem=recv_sem.at[number], device_id=device, device_id_type=MESH,
        )

    def arrive(dst, number):
        pltpu.make_async_copy(dst, dst, recv_sem.at[number]).wait()

    def a_message(o, t):
        slot = a_slot(z, o)
        return message(slot if o else a_ref, slot, A_Z + o * NZ + (t - z + NZ) % NZ, at_z(t))

    def a_arrive(o, t):
        arrive(a_slot(t, o), A_Z + o * NZ + (z - t + NZ) % NZ)

    partner = message(a_ref, a_slot(z, 0), A_PARTNER, dev(flip_h=1))
    b_line = {k: message(b_ref, b_slot(0, y, 1), B_LINE[k], dev(ky=k)) for k in range(1, NY)}

    @pl.when(h == 1)
    def _():
        partner.start()
        tell(A_PARTNER, dev(flip_h=1))

    for t in range(NZ - 1):
        @pl.when(t < z)
        def _():
            a_message(0, t).start()
            tell(A_Z + (t - z + NZ) % NZ, at_z(t))

    for k, c in b_line.items():
        @pl.when(jnp.logical_not(y_later(k)))
        def _():
            c.start()
            tell(B_LINE[k], dev(ky=k))

    for d in X_STEPS:
        @pl.when(jnp.logical_not(x_later(d)))
        def _():
            tell(B_X[d], dev(dx=d))

    @pl.when(core == 0)
    def _():
        tell(B_CORE[0], dev(flip_core=1))

    local = [
        pltpu.make_async_copy(a_ref, a_slot(z, 0), local_sem.at[0]),
        pltpu.make_async_copy(b_ref, b_slot(0, y, 1), local_sem.at[1]),
        pltpu.make_async_copy(mb_ref, ob_ref, local_sem.at[2]),
        pltpu.make_async_copy(ma_ref, oa_ref, local_sem.at[3]),
        pltpu.make_async_copy(wh_ref, oh_ref, local_sem.at[4]),
        pltpu.make_async_copy(wf_ref, of_ref, local_sem.at[5]),
        pltpu.make_async_copy(rr_ref, row_flags, local_sem.at[6]),
        pltpu.make_async_copy(rc_ref, col_flags, local_sem.at[7]),
    ]
    for c in local:
        c.start()

    row_first = (row * (NY * NX * NC) + col) * rows_owned
    col_first = (col * (NZ * NH) + row) * cols_owned
    for i in (2, 3, 6, 7):
        local[i].wait()
    column = col_first + lax.broadcasted_iota(jnp.int32, (a_rows, BLOCK), 0) // 2
    first_block = col_first // BLOCK
    last_block = (col_first + cols_owned - 1) // BLOCK
    for l in range(LAYERS):
        keep_b = 1 - row_flags[l, row_first // BLOCK]
        ob_ref[l] = jnp.where(jnp.full(ob_ref.shape[1:], keep_b) == 0, 0.0, ob_ref[l])
        flag = jnp.where(column // BLOCK == first_block, col_flags[l, first_block], col_flags[l, last_block])
        oa_ref[l] = jnp.where(flag == 1, 0.0, oa_ref[l])

    @pl.when(h == 0)
    def _():
        told(A_PARTNER)
        partner.start()

    for k, c in b_line.items():
        @pl.when(y_later(k))
        def _():
            told(B_LINE[k])
            c.start()

    local[0].wait()
    local[1].wait()
    for k in range(1, NY):
        arrive(b_slot(0, pair(y, k), 1), B_LINE[k])
    b_group = b_slot(0, 0, NY)
    b_near = {d: message(b_group, b_group, B_X[d], dev(dx=d)) for d in X_STEPS}
    for d, c in b_near.items():
        @pl.when(x_later(d))
        def _():
            told(B_X[d if 2 * d == NX else -d])

        c.start()

    @pl.when(core == 1)
    def _():
        told(B_CORE[0])

    b_shared = [message(b_group, b_group, B_CORE[0], dev(flip_core=1))]
    b_shared[0].start()

    def far(t):
        steps = (t - z + NZ) % NZ
        return jnp.logical_and(steps >= FAR, steps <= NZ - FAR)

    def close(t):
        return jnp.logical_and(t != z, jnp.logical_not(far(t)))

    def a_crossing(t):
        slot = a_slot(t, 0)
        return message(slot, slot, A_Z + NZ + (z - t + NZ) % NZ, dev(flip_h=1))

    @pl.when(h == 0)
    def _():
        arrive(a_slot(z, 1), A_PARTNER)
        for t in range(NZ - 1):
            @pl.when(jnp.logical_and(t < z, close(t)))
            def _():
                a_message(1, t).start()

    for t in range(1, NZ):
        @pl.when(t > z)
        def _():
            told(A_Z + (z - t + NZ) % NZ)
            a_message(0, t).start()

            @pl.when(jnp.logical_and(h == 0, close(t)))
            def _():
                a_message(1, t).start()

    @pl.when(h == 1)
    def _():
        arrive(a_slot(z, 1), A_PARTNER)
        for t in range(NZ):
            @pl.when(close(t))
            def _():
                a_message(1, t).start()

    for t in range(NZ):
        @pl.when(far(t))
        def _():
            a_arrive(0, t)
            a_crossing(t).start()

    for d in X_STEPS[::-1]:
        group_b = b_slot(-d, 0, NY)
        arrive(group_b, B_X[d])
        b_shared.append(message(group_b, group_b, B_CORE[d], dev(flip_core=1)))
        b_shared[-1].start()

    for d in (0, *X_STEPS[::-1]):
        arrive(b_slot(-d, 0, NY, 1), B_CORE[d])

    for by in range(NY):
        for bx in range(NX):
            for bc in range(NC):
                at = ((bc * NX + bx) * NY + by) * b_rows
                to = ((by * NX + bx) * NC + bc) * rows_owned
                for l in range(LAYERS):
                    high, low = split(b_all[pl.ds(at + l * rows_owned, rows_owned), :])
                    b_cat[l, pl.ds(to, rows_owned), 0:128] = high
                    b_cat[l, pl.ds(to, rows_owned), 128:256] = high
                    b_cat[l, pl.ds(to, rows_owned), 256:384] = low

    local[4].wait()
    local[5].wait()

    group = 2 * NH * cols_owned
    last = NZ // 2 - 1

    for t in range(NZ):
        @pl.when(close(t))
        def _():
            a_arrive(0, t)

    for j in range(NZ // 2):
        for t in (2 * j, 2 * j + 1):
            @pl.when(t != z)
            def _():
                a_arrive(1, t)

        rows = pl.ds(j * group, group)
        for l, out in enumerate((oh_ref, of_ref)):
            a_rows_l = a_all[pl.ds(j * group * LAYERS + l, group, stride=LAYERS), :]
            if j < last:
                out[rows, :] = merge(out[rows, :], a_rows_l, b_cat[l])
            else:
                a_last[l] = a_rows_l

    sent = [partner, *b_line.values(), *b_near.values(), *b_shared]
    for t in range(NZ):
        @pl.when(t != z)
        def _():
            a_message(0, t).wait_send()

        @pl.when(close(t))
        def _():
            a_message(1, t).wait_send()

        @pl.when(far(t))
        def _():
            a_crossing(t).wait_send()
    for c in sent:
        c.wait_send()


def deliver(
    wh_ref, wf_ref, mb_ref, ma_ref, b_cat, a_last,
    oh_ref, of_ref, ob_ref, oa_ref, last_h, last_f, sems,
):
    group = a_last.shape[1]
    done = wh_ref.shape[0] - group
    first, rest = pl.ds(0, done), pl.ds(done, group)
    copies = [
        pltpu.make_async_copy(wf_ref.at[first], of_ref.at[first], sems.at[0]),
        pltpu.make_async_copy(wh_ref.at[first], oh_ref.at[first], sems.at[1]),
        pltpu.make_async_copy(mb_ref, ob_ref, sems.at[2]),
        pltpu.make_async_copy(ma_ref, oa_ref, sems.at[3]),
    ]
    for c in copies:
        c.start()
    for l, (weight, part, out) in enumerate(((wh_ref, last_h, oh_ref), (wf_ref, last_f, of_ref))):
        part[...] = merge(weight[rest, :], a_last[l], b_cat[l])
        copies.append(pltpu.make_async_copy(part, out.at[rest], sems.at[4 + l]))
        copies[-1].start()
    for c in copies:
        c.wait()


def per_device(
    weight_half, weight_full, adapter_b, adapter_a, moments_b, moments_a, reset_rows, reset_cols
):
    layers, rows_owned, rank = adapter_b.shape
    cols_owned = adapter_a.shape[2]
    wh, wf = weight_half.T, weight_full.T
    b = adapter_b.reshape(layers * rows_owned, rank)
    a = adapter_a.transpose(2, 0, 1).reshape(cols_owned * layers, rank)
    mb = moments_b.reshape(layers, 2 * rows_owned, rank)
    ma = moments_a.transpose(0, 3, 1, 2).reshape(layers, cols_owned * 2, rank)
    shapes = [wh, wf, mb, ma]
    group = 2 * NH * cols_owned
    hbm = pl.BlockSpec(memory_space=pl.ANY)
    vmem = pl.BlockSpec(memory_space=pltpu.VMEM)
    merged = pl.pallas_call(
        gather_merge,
        name="gather_merge",
        out_shape=[pltpu.VMEM(s.shape, s.dtype) for s in shapes] + [
            pltpu.VMEM((layers, NY * NX * NC * rows_owned, 3 * rank), jnp.bfloat16),
            pltpu.VMEM((layers, group, rank), jnp.float32),
        ],
        in_specs=[hbm] * 8,
        out_specs=[vmem] * 6,
        scratch_shapes=[
            pltpu.VMEM((NZ * NH * a.shape[0], rank), jnp.float32),
            pltpu.VMEM((NY * NX * NC * b.shape[0], rank), jnp.float32),
            pltpu.SMEM(reset_rows.shape, jnp.int32),
            pltpu.SMEM(reset_cols.shape, jnp.int32),
            pltpu.SemaphoreType.DMA((MESSAGES,)),
            pltpu.SemaphoreType.DMA((MESSAGES,)),
            pltpu.SemaphoreType.DMA((8,)),
            pltpu.SemaphoreType.REGULAR((B_X[X_STEPS[-1]] + 2,)),
        ],
        compiler_params=pltpu.CompilerParams(
            collective_id=0, has_side_effects=True, vmem_limit_bytes=32 * 1024 * 1024
        ),
    )(*(
        pltpu.with_memory_space_constraint(v, pltpu.HBM)
        for v in (wh, wf, b, a, mb, ma, reset_rows, reset_cols)
    ))
    merged = [pltpu.with_memory_space_constraint(m, pltpu.VMEM) for m in merged]
    oh, of, ob, oa = pl.pallas_call(
        deliver,
        name="deliver",
        out_shape=[jax.ShapeDtypeStruct(s.shape, s.dtype) for s in shapes],
        in_specs=[vmem] * 6,
        out_specs=[hbm] * 4,
        scratch_shapes=[
            pltpu.VMEM((group, wh.shape[1]), wh.dtype),
            pltpu.VMEM((group, wf.shape[1]), wf.dtype),
            pltpu.SemaphoreType.DMA((6,)),
        ],
        compiler_params=pltpu.CompilerParams(vmem_limit_bytes=32 * 1024 * 1024),
    )(*merged)
    oa = oa.reshape(layers, cols_owned, 2, rank).transpose(0, 2, 3, 1)
    return oh.T, of.T, ob.reshape(moments_b.shape), oa


def solution(mesh):
    return jax.shard_map(
        per_device,
        mesh=mesh,
        in_specs=(
            P("row", "col"),
            P("row", "col"),
            P(None, ("row", "col"), None),
            P(None, None, ("col", "row")),
            P(None, None, ("row", "col"), None),
            P(None, None, None, ("col", "row")),
            P(),
            P(),
        ),
        out_specs=(
            P("row", "col"),
            P("row", "col"),
            P(None, None, ("row", "col"), None),
            P(None, None, None, ("col", "row")),
        ),
        check_vma=False,
    )
```

```python
import functools

import jax
import jax.numpy as jnp
from jax import lax
from jax.experimental import pallas as pl
from jax.experimental.pallas import tpu as pltpu
from jax.sharding import PartitionSpec as P

LAYERS = 2
BLOCK = 128
MERGE_SCALE = 0.25
MESH = pl.DeviceIdType.MESH
NZ, NH, NY, NX, NC = 8, 2, 4, 4, 2
X_STEPS = (2, 1, -1)
A_PARTNER = 0
A_Z = 1
B_FIRST = A_Z + NH * NZ
B_LINE = {k: B_FIRST + k for k in range(1, NY)}
B_X = {d: B_FIRST + NY + i for i, d in enumerate(X_STEPS)}
B_CORE = {d: B_FIRST + NY + len(X_STEPS) + i for i, d in enumerate((0, *X_STEPS))}
MESSAGES = B_FIRST + NY + 2 * len(X_STEPS) + 1


def split(v):
    high = v.astype(jnp.bfloat16)
    return high, (v - high.astype(jnp.float32)).astype(jnp.bfloat16)


def merge(weight, a_rows, b_split):
    high, low = split(a_rows)
    update = lax.dot_general(
        jnp.concatenate([high, low, high], axis=1), b_split,
        (((1,), (1,)), ((), ())), preferred_element_type=jnp.float32,
    )
    return (weight.astype(jnp.float32) + MERGE_SCALE * update).astype(weight.dtype)


def gather_merge(
    wh_ref, wf_ref, b_ref, a_ref, mb_ref, ma_ref, rr_ref, rc_ref,
    oh_ref, of_ref, ob_ref, oa_ref, b_cat, a_last,
    a_all, b_all, row_flags, col_flags, send_sem, recv_sem, local_sem, ready_sem,
):
    row, col = lax.axis_index("row"), lax.axis_index("col")
    z, h = row // NH, row % NH
    y, x, core = col // (NX * NC), (col // NC) % NX, col % NC
    a_rows = a_ref.shape[0]
    b_rows = b_ref.shape[0]
    rows_owned = b_rows // LAYERS
    cols_owned = a_rows // LAYERS

    def dev(dz=0, flip_h=0, ky=0, dx=0, flip_core=0):
        tz = (z + dz + NZ) % NZ
        th = (h + flip_h) % NH
        ty = pair(y, ky)
        tx = (x + dx + NX) % NX
        tc = (core + flip_core) % NC
        return (tz * NH + th, (ty * NX + tx) * NC + tc)

    def pair(v, k):
        low, high = v % 2, v // 2
        return ((high + k // 2) % 2) * 2 + (low + k % 2) % 2

    def at_z(t):
        return (t * NH + h, col)

    def a_slot(t, flip_h):
        pos = t * NH + (h + flip_h) % NH
        return a_all.at[pl.ds(pl.multiple_of(pos * a_rows, 8), a_rows), :]

    def b_slot(dx, y_first, y_count, flip_core=0):
        pos = (((core + flip_core) % NC) * NX + (x + dx + NX) % NX) * NY + y_first
        return b_all.at[pl.ds(pl.multiple_of(pos * b_rows, 8), y_count * b_rows), :]

    barrier = pltpu.get_barrier_semaphore()

    def greet(other):
        pl.semaphore_signal(barrier, inc=1, device_id=other, device_id_type=MESH)

    def order_y(v):
        return v + h * (NY - 1 - 2 * v)

    def y_later(k):
        return order_y(pair(y, k)) > order_y(y)

    def x_later(d):
        return (x + d + NX) % NX > x

    def when(condition, action):
        pl.when(condition)(action)

    for t in range(1, NZ):
        when(t > z, functools.partial(greet, at_z(t)))
    when(h == 0, functools.partial(greet, dev(flip_h=1)))
    for k in range(1, NY):
        when(y_later(k), functools.partial(greet, dev(ky=k)))
    for d in X_STEPS:
        when(x_later(d), functools.partial(greet, dev(dx=d)))
    when(core == 1, functools.partial(greet, dev(flip_core=1)))

    def tell(number, other):
        pl.semaphore_signal(ready_sem.at[number], inc=1, device_id=other, device_id_type=MESH)

    def told(number):
        pl.semaphore_wait(ready_sem.at[number], 1)

    greetings = z + h + order_y(y) + x + 1 - core

    @pl.when(greetings > 0)
    def _():
        pl.semaphore_wait(barrier, greetings)

    def message(src, dst, number, device):
        return pltpu.make_async_remote_copy(
            src_ref=src, dst_ref=dst, send_sem=send_sem.at[number],
            recv_sem=recv_sem.at[number], device_id=device, device_id_type=MESH,
        )

    def arrive(dst, number):
        pltpu.make_async_copy(dst, dst, recv_sem.at[number]).wait()

    def a_message(o, t):
        slot = a_slot(z, o)
        return message(slot if o else a_ref, slot, A_Z + o * NZ + (t - z + NZ) % NZ, at_z(t))

    def a_arrive(o, t):
        arrive(a_slot(t, o), A_Z + o * NZ + (z - t + NZ) % NZ)

    partner = message(a_ref, a_slot(z, 0), A_PARTNER, dev(flip_h=1))
    b_line = {k: message(b_ref, b_slot(0, y, 1), B_LINE[k], dev(ky=k)) for k in range(1, NY)}

    @pl.when(h == 1)
    def _():
        partner.start()
        tell(A_PARTNER, dev(flip_h=1))

    for t in range(NZ - 1):
        @pl.when(t < z)
        def _():
            a_message(0, t).start()
            tell(A_Z + (t - z + NZ) % NZ, at_z(t))

    for k, c in b_line.items():
        @pl.when(jnp.logical_not(y_later(k)))
        def _():
            c.start()
            tell(B_LINE[k], dev(ky=k))

    for d in X_STEPS:
        @pl.when(jnp.logical_not(x_later(d)))
        def _():
            tell(B_X[d], dev(dx=d))

    @pl.when(core == 0)
    def _():
        tell(B_CORE[0], dev(flip_core=1))

    local = [
        pltpu.make_async_copy(a_ref, a_slot(z, 0), local_sem.at[0]),
        pltpu.make_async_copy(b_ref, b_slot(0, y, 1), local_sem.at[1]),
        pltpu.make_async_copy(mb_ref, ob_ref, local_sem.at[2]),
        pltpu.make_async_copy(ma_ref, oa_ref, local_sem.at[3]),
        pltpu.make_async_copy(wh_ref, oh_ref, local_sem.at[4]),
        pltpu.make_async_copy(wf_ref, of_ref, local_sem.at[5]),
        pltpu.make_async_copy(rr_ref, row_flags, local_sem.at[6]),
        pltpu.make_async_copy(rc_ref, col_flags, local_sem.at[7]),
    ]
    for c in local:
        c.start()

    row_first = (row * (NY * NX * NC) + col) * rows_owned
    col_first = (col * (NZ * NH) + row) * cols_owned
    for i in (2, 3, 6, 7):
        local[i].wait()
    column = col_first + lax.broadcasted_iota(jnp.int32, (a_rows, BLOCK), 0) // 2
    first_block = col_first // BLOCK
    last_block = (col_first + cols_owned - 1) // BLOCK
    for l in range(LAYERS):
        keep_b = 1 - row_flags[l, row_first // BLOCK]
        ob_ref[l] = jnp.where(jnp.full(ob_ref.shape[1:], keep_b) == 0, 0.0, ob_ref[l])
        flag = jnp.where(column // BLOCK == first_block, col_flags[l, first_block], col_flags[l, last_block])
        oa_ref[l] = jnp.where(flag == 1, 0.0, oa_ref[l])

    @pl.when(h == 0)
    def _():
        told(A_PARTNER)
        partner.start()

    for k, c in b_line.items():
        @pl.when(y_later(k))
        def _():
            told(B_LINE[k])
            c.start()

    local[0].wait()
    local[1].wait()
    for k in range(1, NY):
        arrive(b_slot(0, pair(y, k), 1), B_LINE[k])
    b_group = b_slot(0, 0, NY)
    b_near = {d: message(b_group, b_group, B_X[d], dev(dx=d)) for d in X_STEPS}
    for d, c in b_near.items():
        @pl.when(x_later(d))
        def _():
            told(B_X[d if 2 * d == NX else -d])

        c.start()

    @pl.when(core == 1)
    def _():
        told(B_CORE[0])

    b_shared = [message(b_group, b_group, B_CORE[0], dev(flip_core=1))]
    b_shared[0].start()

    def crosses(origin, to):
        steps = (origin - to + NZ) % NZ
        return jnp.logical_or(
            jnp.logical_or(steps == 5, steps == 4), jnp.logical_and(steps == 3, core == 1)
        )

    def sends_to(t):
        return jnp.logical_and(t != z, jnp.logical_not(crosses(z, t)))

    def a_crossing(t):
        slot = a_slot(t, 0)
        return message(slot, slot, A_Z + NZ + (z - t + NZ) % NZ, dev(flip_h=1))

    @pl.when(h == 0)
    def _():
        arrive(a_slot(z, 1), A_PARTNER)
        for t in range(NZ - 1):
            @pl.when(jnp.logical_and(t < z, sends_to(t)))
            def _():
                a_message(1, t).start()

    for t in range(1, NZ):
        @pl.when(t > z)
        def _():
            told(A_Z + (z - t + NZ) % NZ)
            a_message(0, t).start()

            @pl.when(jnp.logical_and(h == 0, sends_to(t)))
            def _():
                a_message(1, t).start()

    @pl.when(h == 1)
    def _():
        arrive(a_slot(z, 1), A_PARTNER)
        for t in range(NZ):
            @pl.when(sends_to(t))
            def _():
                a_message(1, t).start()

    for t in range(NZ):
        @pl.when(crosses(t, z))
        def _():
            a_arrive(0, t)
            a_crossing(t).start()

    for d in X_STEPS[::-1]:
        group_b = b_slot(-d, 0, NY)
        arrive(group_b, B_X[d])
        b_shared.append(message(group_b, group_b, B_CORE[d], dev(flip_core=1)))
        b_shared[-1].start()

    for d in (0, *X_STEPS[::-1]):
        arrive(b_slot(-d, 0, NY, 1), B_CORE[d])

    for by in range(NY):
        for bx in range(NX):
            for bc in range(NC):
                at = ((bc * NX + bx) * NY + by) * b_rows
                to = ((by * NX + bx) * NC + bc) * rows_owned
                for l in range(LAYERS):
                    high, low = split(b_all[pl.ds(at + l * rows_owned, rows_owned), :])
                    b_cat[l, pl.ds(to, rows_owned), 0:128] = high
                    b_cat[l, pl.ds(to, rows_owned), 128:256] = high
                    b_cat[l, pl.ds(to, rows_owned), 256:384] = low

    local[4].wait()
    local[5].wait()

    group = 2 * NH * cols_owned
    last = NZ // 2 - 1

    for t in range(NZ):
        @pl.when(jnp.logical_and(t != z, jnp.logical_not(crosses(t, z))))
        def _():
            a_arrive(0, t)

    for j in range(NZ // 2):
        for t in (2 * j, 2 * j + 1):
            @pl.when(t != z)
            def _():
                a_arrive(1, t)

        rows = pl.ds(j * group, group)
        for l, out in enumerate((oh_ref, of_ref)):
            a_rows_l = a_all[pl.ds(j * group * LAYERS + l, group, stride=LAYERS), :]
            if j < last:
                out[rows, :] = merge(out[rows, :], a_rows_l, b_cat[l])
            else:
                a_last[l] = a_rows_l

    sent = [partner, *b_line.values(), *b_near.values(), *b_shared]
    for t in range(NZ):
        @pl.when(t != z)
        def _():
            a_message(0, t).wait_send()

        @pl.when(sends_to(t))
        def _():
            a_message(1, t).wait_send()

        @pl.when(crosses(t, z))
        def _():
            a_crossing(t).wait_send()
    for c in sent:
        c.wait_send()


def deliver(
    wh_ref, wf_ref, mb_ref, ma_ref, b_cat, a_last,
    oh_ref, of_ref, ob_ref, oa_ref, last_h, last_f, sems,
):
    group = a_last.shape[1]
    done = wh_ref.shape[0] - group
    first, rest = pl.ds(0, done), pl.ds(done, group)
    copies = [
        pltpu.make_async_copy(wf_ref.at[first], of_ref.at[first], sems.at[0]),
        pltpu.make_async_copy(wh_ref.at[first], oh_ref.at[first], sems.at[1]),
        pltpu.make_async_copy(mb_ref, ob_ref, sems.at[2]),
        pltpu.make_async_copy(ma_ref, oa_ref, sems.at[3]),
    ]
    for c in copies:
        c.start()
    for l, (weight, part, out) in enumerate(((wh_ref, last_h, oh_ref), (wf_ref, last_f, of_ref))):
        part[...] = merge(weight[rest, :], a_last[l], b_cat[l])
        copies.append(pltpu.make_async_copy(part, out.at[rest], sems.at[4 + l]))
        copies[-1].start()
    for c in copies:
        c.wait()


def per_device(
    weight_half, weight_full, adapter_b, adapter_a, moments_b, moments_a, reset_rows, reset_cols
):
    layers, rows_owned, rank = adapter_b.shape
    cols_owned = adapter_a.shape[2]
    wh, wf = weight_half.T, weight_full.T
    b = adapter_b.reshape(layers * rows_owned, rank)
    a = adapter_a.transpose(2, 0, 1).reshape(cols_owned * layers, rank)
    mb = moments_b.reshape(layers, 2 * rows_owned, rank)
    ma = moments_a.transpose(0, 3, 1, 2).reshape(layers, cols_owned * 2, rank)
    shapes = [wh, wf, mb, ma]
    group = 2 * NH * cols_owned
    hbm = pl.BlockSpec(memory_space=pl.ANY)
    vmem = pl.BlockSpec(memory_space=pltpu.VMEM)
    merged = pl.pallas_call(
        gather_merge,
        name="gather_merge",
        out_shape=[pltpu.VMEM(s.shape, s.dtype) for s in shapes] + [
            pltpu.VMEM((layers, NY * NX * NC * rows_owned, 3 * rank), jnp.bfloat16),
            pltpu.VMEM((layers, group, rank), jnp.float32),
        ],
        in_specs=[hbm] * 8,
        out_specs=[vmem] * 6,
        scratch_shapes=[
            pltpu.VMEM((NZ * NH * a.shape[0], rank), jnp.float32),
            pltpu.VMEM((NY * NX * NC * b.shape[0], rank), jnp.float32),
            pltpu.SMEM(reset_rows.shape, jnp.int32),
            pltpu.SMEM(reset_cols.shape, jnp.int32),
            pltpu.SemaphoreType.DMA((MESSAGES,)),
            pltpu.SemaphoreType.DMA((MESSAGES,)),
            pltpu.SemaphoreType.DMA((8,)),
            pltpu.SemaphoreType.REGULAR((B_X[X_STEPS[-1]] + 2,)),
        ],
        compiler_params=pltpu.CompilerParams(
            collective_id=0, has_side_effects=True, vmem_limit_bytes=32 * 1024 * 1024
        ),
    )(*(
        pltpu.with_memory_space_constraint(v, pltpu.HBM)
        for v in (wh, wf, b, a, mb, ma, reset_rows, reset_cols)
    ))
    merged = [pltpu.with_memory_space_constraint(m, pltpu.VMEM) for m in merged]
    oh, of, ob, oa = pl.pallas_call(
        deliver,
        name="deliver",
        out_shape=[jax.ShapeDtypeStruct(s.shape, s.dtype) for s in shapes],
        in_specs=[vmem] * 6,
        out_specs=[hbm] * 4,
        scratch_shapes=[
            pltpu.VMEM((group, wh.shape[1]), wh.dtype),
            pltpu.VMEM((group, wf.shape[1]), wf.dtype),
            pltpu.SemaphoreType.DMA((6,)),
        ],
        compiler_params=pltpu.CompilerParams(vmem_limit_bytes=32 * 1024 * 1024),
    )(*merged)
    oa = oa.reshape(layers, cols_owned, 2, rank).transpose(0, 2, 3, 1)
    return oh.T, of.T, ob.reshape(moments_b.shape), oa


def solution(mesh):
    return jax.shard_map(
        per_device,
        mesh=mesh,
        in_specs=(
            P("row", "col"),
            P("row", "col"),
            P(None, ("row", "col"), None),
            P(None, None, ("col", "row")),
            P(None, None, ("row", "col"), None),
            P(None, None, None, ("col", "row")),
            P(),
            P(),
        ),
        out_specs=(
            P("row", "col"),
            P("row", "col"),
            P(None, None, ("row", "col"), None),
            P(None, None, None, ("col", "row")),
        ),
        check_vma=False,
    )
```

```python
import functools

import jax
import jax.numpy as jnp
from jax import lax
from jax.experimental import pallas as pl
from jax.experimental.pallas import tpu as pltpu
from jax.sharding import PartitionSpec as P

LAYERS = 2
BLOCK = 128
MERGE_SCALE = 0.25
MESH = pl.DeviceIdType.MESH
NZ, NH, NY, NX, NC = 8, 2, 4, 4, 2
X_STEPS = (2, 1, -1)
A_PARTNER = 0
A_Z = 1
B_FIRST = A_Z + NH * NZ
B_LINE = {k: B_FIRST + k for k in range(1, NY)}
B_X = {d: B_FIRST + NY + i for i, d in enumerate(X_STEPS)}
B_CORE = {d: B_FIRST + NY + len(X_STEPS) + i for i, d in enumerate((0, *X_STEPS))}
MESSAGES = B_FIRST + NY + 2 * len(X_STEPS) + 1


def split(v):
    high = v.astype(jnp.bfloat16)
    return high, (v - high.astype(jnp.float32)).astype(jnp.bfloat16)


def merge(weight, a_rows, b_split):
    high, low = split(a_rows)
    update = lax.dot_general(
        jnp.concatenate([high, low, high], axis=1), b_split,
        (((1,), (1,)), ((), ())), preferred_element_type=jnp.float32,
    )
    return (weight.astype(jnp.float32) + MERGE_SCALE * update).astype(weight.dtype)


def gather_merge(
    wh_ref, wf_ref, b_ref, a_ref, mb_ref, ma_ref, rr_ref, rc_ref,
    oh_ref, of_ref, ob_ref, oa_ref, b_cat, a_last,
    a_all, b_all, row_flags, col_flags, send_sem, recv_sem, local_sem, ready_sem,
):
    row, col = lax.axis_index("row"), lax.axis_index("col")
    z, h = row // NH, row % NH
    y, x, core = col // (NX * NC), (col // NC) % NX, col % NC
    a_rows = a_ref.shape[0]
    b_rows = b_ref.shape[0]
    rows_owned = b_rows // LAYERS
    cols_owned = a_rows // LAYERS

    def dev(dz=0, flip_h=0, ky=0, dx=0, flip_core=0):
        tz = (z + dz + NZ) % NZ
        th = (h + flip_h) % NH
        ty = pair(y, ky)
        tx = (x + dx + NX) % NX
        tc = (core + flip_core) % NC
        return (tz * NH + th, (ty * NX + tx) * NC + tc)

    def pair(v, k):
        low, high = v % 2, v // 2
        return ((high + k // 2) % 2) * 2 + (low + k % 2) % 2

    def at_z(t):
        return (t * NH + h, col)

    def a_slot(t, flip_h):
        pos = t * NH + (h + flip_h) % NH
        return a_all.at[pl.ds(pl.multiple_of(pos * a_rows, 8), a_rows), :]

    def b_slot(dx, y_first, y_count, flip_core=0):
        pos = (((core + flip_core) % NC) * NX + (x + dx + NX) % NX) * NY + y_first
        return b_all.at[pl.ds(pl.multiple_of(pos * b_rows, 8), y_count * b_rows), :]

    barrier = pltpu.get_barrier_semaphore()

    def greet(other):
        pl.semaphore_signal(barrier, inc=1, device_id=other, device_id_type=MESH)

    def order_y(v):
        return v + h * (NY - 1 - 2 * v)

    def y_later(k):
        return order_y(pair(y, k)) > order_y(y)

    def x_later(d):
        return (x + d + NX) % NX > x

    def when(condition, action):
        pl.when(condition)(action)

    for t in range(1, NZ):
        when(t > z, functools.partial(greet, at_z(t)))
    when(h == 0, functools.partial(greet, dev(flip_h=1)))
    for k in range(1, NY):
        when(y_later(k), functools.partial(greet, dev(ky=k)))
    for d in X_STEPS:
        when(x_later(d), functools.partial(greet, dev(dx=d)))
    when(core == 1, functools.partial(greet, dev(flip_core=1)))

    def tell(number, other):
        pl.semaphore_signal(ready_sem.at[number], inc=1, device_id=other, device_id_type=MESH)

    def told(number):
        pl.semaphore_wait(ready_sem.at[number], 1)

    greetings = z + h + order_y(y) + x + 1 - core

    @pl.when(greetings > 0)
    def _():
        pl.semaphore_wait(barrier, greetings)

    def message(src, dst, number, device):
        return pltpu.make_async_remote_copy(
            src_ref=src, dst_ref=dst, send_sem=send_sem.at[number],
            recv_sem=recv_sem.at[number], device_id=device, device_id_type=MESH,
        )

    def arrive(dst, number):
        pltpu.make_async_copy(dst, dst, recv_sem.at[number]).wait()

    def a_message(o, t):
        slot = a_slot(z, o)
        return message(slot if o else a_ref, slot, A_Z + o * NZ + (t - z + NZ) % NZ, at_z(t))

    def a_arrive(o, t):
        arrive(a_slot(t, o), A_Z + o * NZ + (z - t + NZ) % NZ)

    partner = message(a_ref, a_slot(z, 0), A_PARTNER, dev(flip_h=1))
    b_line = {k: message(b_ref, b_slot(0, y, 1), B_LINE[k], dev(ky=k)) for k in range(1, NY)}

    @pl.when(h == 1)
    def _():
        partner.start()
        tell(A_PARTNER, dev(flip_h=1))

    for t in range(NZ - 1):
        @pl.when(t < z)
        def _():
            a_message(0, t).start()
            tell(A_Z + (t - z + NZ) % NZ, at_z(t))

    for k, c in b_line.items():
        @pl.when(jnp.logical_not(y_later(k)))
        def _():
            c.start()
            tell(B_LINE[k], dev(ky=k))

    for d in X_STEPS:
        @pl.when(jnp.logical_not(x_later(d)))
        def _():
            tell(B_X[d], dev(dx=d))

    @pl.when(core == 0)
    def _():
        tell(B_CORE[0], dev(flip_core=1))

    local = [
        pltpu.make_async_copy(a_ref, a_slot(z, 0), local_sem.at[0]),
        pltpu.make_async_copy(b_ref, b_slot(0, y, 1), local_sem.at[1]),
        pltpu.make_async_copy(mb_ref, ob_ref, local_sem.at[2]),
        pltpu.make_async_copy(ma_ref, oa_ref, local_sem.at[3]),
        pltpu.make_async_copy(wh_ref, oh_ref, local_sem.at[4]),
        pltpu.make_async_copy(wf_ref, of_ref, local_sem.at[5]),
        pltpu.make_async_copy(rr_ref, row_flags, local_sem.at[6]),
        pltpu.make_async_copy(rc_ref, col_flags, local_sem.at[7]),
    ]
    for c in local:
        c.start()

    row_first = (row * (NY * NX * NC) + col) * rows_owned
    col_first = (col * (NZ * NH) + row) * cols_owned
    for i in (2, 3, 6, 7):
        local[i].wait()
    column = col_first + lax.broadcasted_iota(jnp.int32, (a_rows, BLOCK), 0) // 2
    first_block = col_first // BLOCK
    last_block = (col_first + cols_owned - 1) // BLOCK
    for l in range(LAYERS):
        keep_b = 1 - row_flags[l, row_first // BLOCK]
        ob_ref[l] = jnp.where(jnp.full(ob_ref.shape[1:], keep_b) == 0, 0.0, ob_ref[l])
        flag = jnp.where(column // BLOCK == first_block, col_flags[l, first_block], col_flags[l, last_block])
        oa_ref[l] = jnp.where(flag == 1, 0.0, oa_ref[l])

    @pl.when(h == 0)
    def _():
        told(A_PARTNER)
        partner.start()

    for k, c in b_line.items():
        @pl.when(y_later(k))
        def _():
            told(B_LINE[k])
            c.start()

    local[0].wait()
    local[1].wait()
    for k in range(1, NY):
        arrive(b_slot(0, pair(y, k), 1), B_LINE[k])
    b_group = b_slot(0, 0, NY)
    b_near = {d: message(b_group, b_group, B_X[d], dev(dx=d)) for d in X_STEPS}
    for d, c in b_near.items():
        @pl.when(x_later(d))
        def _():
            told(B_X[d if 2 * d == NX else -d])

        c.start()

    @pl.when(core == 1)
    def _():
        told(B_CORE[0])

    b_shared = [message(b_group, b_group, B_CORE[0], dev(flip_core=1))]
    b_shared[0].start()

    def crosses(origin, to):
        steps = (origin - to + NZ) % NZ
        return jnp.logical_or(
            jnp.logical_or(steps == 5, steps == 4), jnp.logical_and(steps == 3, core == 1)
        )

    def sends_to(t):
        return jnp.logical_and(t != z, jnp.logical_not(crosses(z, t)))

    def a_crossing(t):
        slot = a_slot(t, 0)
        return message(slot, slot, A_Z + NZ + (z - t + NZ) % NZ, dev(flip_h=1))

    for t in range(1, NZ):
        @pl.when(t > z)
        def _():
            told(A_Z + (z - t + NZ) % NZ)
            a_message(0, t).start()

    arrive(a_slot(z, 1), A_PARTNER)
    for t in range(NZ):
        @pl.when(sends_to(t))
        def _():
            a_message(1, t).start()

    for t in range(NZ):
        @pl.when(crosses(t, z))
        def _():
            a_arrive(0, t)
            a_crossing(t).start()

    for d in X_STEPS[::-1]:
        group_b = b_slot(-d, 0, NY)
        arrive(group_b, B_X[d])
        b_shared.append(message(group_b, group_b, B_CORE[d], dev(flip_core=1)))
        b_shared[-1].start()

    for d in (0, *X_STEPS[::-1]):
        arrive(b_slot(-d, 0, NY, 1), B_CORE[d])

    for by in range(NY):
        for bx in range(NX):
            for bc in range(NC):
                at = ((bc * NX + bx) * NY + by) * b_rows
                to = ((by * NX + bx) * NC + bc) * rows_owned
                for l in range(LAYERS):
                    high, low = split(b_all[pl.ds(at + l * rows_owned, rows_owned), :])
                    b_cat[l, pl.ds(to, rows_owned), 0:128] = high
                    b_cat[l, pl.ds(to, rows_owned), 128:256] = high
                    b_cat[l, pl.ds(to, rows_owned), 256:384] = low

    local[4].wait()
    local[5].wait()

    group = 2 * NH * cols_owned
    last = NZ // 2 - 1

    for t in range(NZ):
        @pl.when(jnp.logical_and(t != z, jnp.logical_not(crosses(t, z))))
        def _():
            a_arrive(0, t)

    for j in range(NZ // 2):
        for t in (2 * j, 2 * j + 1):
            @pl.when(t != z)
            def _():
                a_arrive(1, t)

        rows = pl.ds(j * group, group)
        for l, out in enumerate((oh_ref, of_ref)):
            a_rows_l = a_all[pl.ds(j * group * LAYERS + l, group, stride=LAYERS), :]
            if j < last:
                out[rows, :] = merge(out[rows, :], a_rows_l, b_cat[l])
            else:
                a_last[l] = a_rows_l

    sent = [partner, *b_line.values(), *b_near.values(), *b_shared]
    for t in range(NZ):
        @pl.when(t != z)
        def _():
            a_message(0, t).wait_send()

        @pl.when(sends_to(t))
        def _():
            a_message(1, t).wait_send()

        @pl.when(crosses(t, z))
        def _():
            a_crossing(t).wait_send()
    for c in sent:
        c.wait_send()


def deliver(
    wh_ref, wf_ref, mb_ref, ma_ref, b_cat, a_last,
    oh_ref, of_ref, ob_ref, oa_ref, last_h, last_f, sems,
):
    group = a_last.shape[1]
    done = wh_ref.shape[0] - group
    first, rest = pl.ds(0, done), pl.ds(done, group)
    copies = [
        pltpu.make_async_copy(wf_ref.at[first], of_ref.at[first], sems.at[0]),
        pltpu.make_async_copy(wh_ref.at[first], oh_ref.at[first], sems.at[1]),
        pltpu.make_async_copy(mb_ref, ob_ref, sems.at[2]),
        pltpu.make_async_copy(ma_ref, oa_ref, sems.at[3]),
    ]
    for c in copies:
        c.start()
    for l, (weight, part, out) in enumerate(((wh_ref, last_h, oh_ref), (wf_ref, last_f, of_ref))):
        part[...] = merge(weight[rest, :], a_last[l], b_cat[l])
        copies.append(pltpu.make_async_copy(part, out.at[rest], sems.at[4 + l]))
        copies[-1].start()
    for c in copies:
        c.wait()


def per_device(
    weight_half, weight_full, adapter_b, adapter_a, moments_b, moments_a, reset_rows, reset_cols
):
    layers, rows_owned, rank = adapter_b.shape
    cols_owned = adapter_a.shape[2]
    wh, wf = weight_half.T, weight_full.T
    b = adapter_b.reshape(layers * rows_owned, rank)
    a = adapter_a.transpose(2, 0, 1).reshape(cols_owned * layers, rank)
    mb = moments_b.reshape(layers, 2 * rows_owned, rank)
    ma = moments_a.transpose(0, 3, 1, 2).reshape(layers, cols_owned * 2, rank)
    shapes = [wh, wf, mb, ma]
    group = 2 * NH * cols_owned
    hbm = pl.BlockSpec(memory_space=pl.ANY)
    vmem = pl.BlockSpec(memory_space=pltpu.VMEM)
    merged = pl.pallas_call(
        gather_merge,
        name="gather_merge",
        out_shape=[pltpu.VMEM(s.shape, s.dtype) for s in shapes] + [
            pltpu.VMEM((layers, NY * NX * NC * rows_owned, 3 * rank), jnp.bfloat16),
            pltpu.VMEM((layers, group, rank), jnp.float32),
        ],
        in_specs=[hbm] * 8,
        out_specs=[vmem] * 6,
        scratch_shapes=[
            pltpu.VMEM((NZ * NH * a.shape[0], rank), jnp.float32),
            pltpu.VMEM((NY * NX * NC * b.shape[0], rank), jnp.float32),
            pltpu.SMEM(reset_rows.shape, jnp.int32),
            pltpu.SMEM(reset_cols.shape, jnp.int32),
            pltpu.SemaphoreType.DMA((MESSAGES,)),
            pltpu.SemaphoreType.DMA((MESSAGES,)),
            pltpu.SemaphoreType.DMA((8,)),
            pltpu.SemaphoreType.REGULAR((B_X[X_STEPS[-1]] + 2,)),
        ],
        compiler_params=pltpu.CompilerParams(
            collective_id=0, has_side_effects=True, vmem_limit_bytes=32 * 1024 * 1024
        ),
    )(*(
        pltpu.with_memory_space_constraint(v, pltpu.HBM)
        for v in (wh, wf, b, a, mb, ma, reset_rows, reset_cols)
    ))
    merged = [pltpu.with_memory_space_constraint(m, pltpu.VMEM) for m in merged]
    oh, of, ob, oa = pl.pallas_call(
        deliver,
        name="deliver",
        out_shape=[jax.ShapeDtypeStruct(s.shape, s.dtype) for s in shapes],
        in_specs=[vmem] * 6,
        out_specs=[hbm] * 4,
        scratch_shapes=[
            pltpu.VMEM((group, wh.shape[1]), wh.dtype),
            pltpu.VMEM((group, wf.shape[1]), wf.dtype),
            pltpu.SemaphoreType.DMA((6,)),
        ],
        compiler_params=pltpu.CompilerParams(vmem_limit_bytes=32 * 1024 * 1024),
    )(*merged)
    oa = oa.reshape(layers, cols_owned, 2, rank).transpose(0, 2, 3, 1)
    return oh.T, of.T, ob.reshape(moments_b.shape), oa


def solution(mesh):
    return jax.shard_map(
        per_device,
        mesh=mesh,
        in_specs=(
            P("row", "col"),
            P("row", "col"),
            P(None, ("row", "col"), None),
            P(None, None, ("col", "row")),
            P(None, None, ("row", "col"), None),
            P(None, None, None, ("col", "row")),
            P(),
            P(),
        ),
        out_specs=(
            P("row", "col"),
            P("row", "col"),
            P(None, None, ("row", "col"), None),
            P(None, None, None, ("col", "row")),
        ),
        check_vma=False,
    )
```
